32 devices in a mesh: dp: 4 (over y, x), row: 4 (over z), col: 2 (over core).
Axes of the slice: x: 2, y: 2, z: 4, core: 2. Of those that a mesh axis runs over, the one named last changes fastest.
Arguments:
- activations: bfloat16 [7168, 6144], P(('dp', 'row'), 'col'), may hold values from -6 to 6
- cotangent: bfloat16 [7168, 12288], P(('dp', 'col'), 'row'), may hold values from -6 to 6
- preact: bfloat16 [7168, 12288], P(('dp', 'col'), 'row'), may hold values from -6 to 6
- weight: bfloat16 [6144, 12288], P('col', 'row'), may hold values from -0.078125 to 0.078125
- adapter_input_weight: bfloat16 [3, 32, 6144], P(None, None, 'col'), may hold values from -0.078125 to 0.078125
- adapter_output_weight: bfloat16 [3, 32, 12288], P(None, None, 'row'), may hold values from -1 to 1
- owner: int32 [4], replicated, may hold values from 0 to 2, as said below
Outputs:
- grad_input: bfloat16 [7168, 6144], P(('dp', 'row'), 'col')
- grad_weight: bfloat16 [6144, 12288], P('col', 'row')
- lora_in_grad: float32 [3, 32, 6144], P(None, None, 'col')
- lora_out_grad: float32 [3, 32, 12288], P(None, None, 'row')
The draws below stay inside these ranges and needn't reach their ends.
Inputs may be any that keep to these rules, and one draw needn't show every extreme that they name: `owner`: customer of each index of dp; each of the 3 customers owns at least one index, so some own several.
All inputs are finite; a program needn't handle non-finite values.
Results may differ from the reference program's by a relative error of at most 0.024.
Values may be sent and summed in bfloat16 or wider, within the bound.
No kernel may reach another device: no remote copies, remote signals or barrier semaphores. Data moves between devices by JAX's collectives and lax.ppermute only.
A program may use at most 192 MiB of HBM per device.

```python
import jax
import jax.numpy as jnp
from jax import lax

MODEL_WIDTH = 6144
HIDDEN_HALF = 12288
ADAPTER_RANK = 32
CUSTOMER_COUNT = 3
TOK_GROUP = 1792
TOKENS = 7168
N_DP = 4
N_ROW = 4


def draw_owner(key, part):
    key = jax.random.fold_in(key, 7)
    return (jax.random.permutation(key, N_DP) % CUSTOMER_COUNT).astype(jnp.int32)


def block_scale(stream_key, dims, shards, least, top_value):
    loudness = 1.0
    for dim, parts in shards:
        heights = jax.random.uniform(jax.random.fold_in(jax.random.fold_in(stream_key, 6), dim), (parts,), jnp.float32, least / len(shards), top_value / len(shards))
        loudness = loudness * jnp.repeat(jnp.exp(heights), dims[dim] // parts).reshape((-1,) + (1,) * (len(dims) - 1 - dim))
    return loudness


def normal_values(stream_key, extent, deviation, bound, pieces=(), kind=jnp.bfloat16):
    factor_of = block_scale(stream_key, extent, pieces, -0.22, 0.18) if pieces else 1.0
    entries = jax.random.normal(stream_key, extent, jnp.float32) * deviation * factor_of
    return jnp.minimum(jnp.maximum(entries, -bound), bound).astype(kind)


def setup_inputs(seed: int = 0) -> dict:
    seeds = jax.random.split(jax.random.key(seed), 8)
    return {
        "activations": normal_values(seeds[0], (TOKENS, MODEL_WIDTH), 1.0, 6.0, ((0, 16), (1, 2))),
        "cotangent": normal_values(seeds[1], (TOKENS, HIDDEN_HALF), 1.0, 6.0, ((0, 8), (1, 4))),
        "preact": normal_values(seeds[2], (TOKENS, HIDDEN_HALF), 1.0, 6.0, ((0, 8), (1, 4))),
        "weight": normal_values(seeds[3], (MODEL_WIDTH, HIDDEN_HALF), MODEL_WIDTH ** -0.5, 0.078125, ((0, 2), (1, 4))),
        "adapter_input_weight": normal_values(seeds[4], (CUSTOMER_COUNT, ADAPTER_RANK, MODEL_WIDTH), MODEL_WIDTH ** -0.5, 0.078125, ((2, 2),)),
        "adapter_output_weight": normal_values(seeds[5], (CUSTOMER_COUNT, ADAPTER_RANK, HIDDEN_HALF), ADAPTER_RANK ** -0.5, 1.0, ((2, 4),)),
        "owner": draw_owner(jax.random.fold_in(seeds[7], 71), 0),
    }


adapter_scale_factor = 2.0


def gelu_slope(value):
    return 0.5 * (1.0 + lax.erf(value * 0.7071067811865476)) + value * jnp.exp(-0.5 * value * value) * 0.3989422804014327


def rounded(value):
    return lax.optimization_barrier(value.astype(jnp.bfloat16)).astype(jnp.float32)


def reference(activations, cotangent, preact, weight, adapter_input_weight, adapter_output_weight, owner):
    block_width = HIDDEN_HALF // N_ROW
    grad_pre = (cotangent.astype(jnp.float32) * gelu_slope(preact.astype(jnp.float32))).astype(jnp.bfloat16)
    weight_total = jnp.zeros((MODEL_WIDTH, HIDDEN_HALF), jnp.float32)
    in_total = jnp.zeros((CUSTOMER_COUNT, ADAPTER_RANK, MODEL_WIDTH), jnp.float32)
    out_total = jnp.zeros((CUSTOMER_COUNT, ADAPTER_RANK, HIDDEN_HALF), jnp.float32)
    outputs_list = []
    for group_index in range(N_DP):
        first = group_index * TOK_GROUP
        grouped_activation_rows = activations[first:first + TOK_GROUP]
        grouped_gradient_rows = grad_pre[first:first + TOK_GROUP]
        client_index = owner[group_index]
        rank_down_result = adapter_input_weight[client_index]
        rank_upward_result = adapter_output_weight[client_index]
        wide_down_result = rank_down_result.astype(jnp.float32)
        weight_total = weight_total + rounded(jnp.dot(grouped_activation_rows.T, grouped_gradient_rows, preferred_element_type=jnp.float32))
        rank_activation = jnp.dot(grouped_activation_rows, rank_down_result.T, preferred_element_type=jnp.float32).astype(jnp.bfloat16)
        low_sum = jnp.zeros((TOK_GROUP, ADAPTER_RANK), jnp.float32)
        input_sum = jnp.zeros((TOK_GROUP, MODEL_WIDTH), jnp.float32)
        for row_block in range(N_ROW):
            lower = row_block * block_width
            grad_piece = grouped_gradient_rows[:, lower:lower + block_width]
            rank_portion = jnp.dot(grad_piece, rank_upward_result[:, lower:lower + block_width].T, preferred_element_type=jnp.float32)
            incomplete_term = jnp.dot(grad_piece, weight[:, lower:lower + block_width].T, preferred_element_type=jnp.float32)
            incomplete_term = incomplete_term + adapter_scale_factor * jnp.dot(rank_portion, wide_down_result, precision=lax.Precision.HIGHEST)
            input_sum = input_sum + rounded(incomplete_term)
            low_sum = low_sum + rounded(rank_portion)
        outputs_list.append(input_sum.astype(jnp.bfloat16))
        rank_gradient = low_sum.astype(jnp.bfloat16)
        owner_mask = (jnp.arange(CUSTOMER_COUNT) == client_index).astype(jnp.float32)
        input_adapter_term = adapter_scale_factor * jnp.dot(rank_gradient.T, grouped_activation_rows, preferred_element_type=jnp.float32)
        output_adapter_term = adapter_scale_factor * jnp.dot(rank_activation.T, grouped_gradient_rows, preferred_element_type=jnp.float32)
        in_total = in_total + owner_mask[:, None, None] * input_adapter_term[None]
        out_total = out_total + owner_mask[:, None, None] * output_adapter_term[None]
    grad_input = jnp.concatenate(outputs_list, axis=0)
    return grad_input, weight_total.astype(jnp.bfloat16), in_total, out_total
```

```python
import jax
import jax.numpy as jnp
from jax import lax
from jax.experimental import pallas as pl
from jax.experimental.pallas import tpu as pltpu
from jax.sharding import PartitionSpec as P

CUSTOMER_COUNT = 3
VMEM_LIMIT = 60 * 1024 * 1024
CHUNKS = (2, 2, 3, 3, 2)
LOW_CHUNK = 2

adapter_scale_factor = 2.0


def gelu_slope(value):
    return (
        0.5 * (1.0 + lax.erf(value * 0.7071067811865476))
        + value * jnp.exp(-0.5 * value * value) * 0.3989422804014327
    )


def cost(flops, moved):
    return pl.CostEstimate(flops=3 * flops, bytes_accessed=3 * moved, transcendentals=0)


def anywhere(count):
    return [pl.BlockSpec(memory_space=pl.ANY)] * count


def cut_columns(source, start, width, more, earlier):
    rows = source.shape[0]
    total = width + sum(piece.shape[1] for piece in more)

    def body(source_ref, *refs):
        out, one = refs[-2:]
        one[...] = jnp.ones_like(one)
        out[:, :width] = source_ref[:, start : start + width]
        if more:
            out[:, width:] = refs[0][...]

    return pl.pallas_call(
        body,
        grid=(1,),
        in_specs=[pl.BlockSpec(source.shape, lambda step: (0, 0))]
        + [pl.BlockSpec(piece.shape, lambda step: (0, 0)) for piece in more]
        + anywhere(len(earlier)),
        out_specs=[
            pl.BlockSpec((rows, total), lambda step: (0, 0)),
            pl.BlockSpec((8, 128), lambda step: (0, 0)),
        ],
        out_shape=[
            jax.ShapeDtypeStruct((rows, total), source.dtype),
            jax.ShapeDtypeStruct((8, 128), jnp.float32),
        ],
        compiler_params=pltpu.CompilerParams(vmem_limit_bytes=VMEM_LIMIT),
        cost_estimate=cost(0, 4 * rows * total),
        name="cut_columns",
    )(source, *more, *earlier)


def weight_chunk(choice, act, own, other, features, rank, extra, earlier):
    total = act.shape[1]
    half, hidden = own.shape
    cut = hidden // 8
    block = 2 * cut
    below = sum(CUSTOMER_COUNT * blocks.shape[1] for blocks in extra)
    shapes = [(features + below, block)] * 2 + [(features + below, cut)] * 4
    more = [(8, rank, cut)] if rank else []

    def body(choice_ref, *refs):
        (act_ref, own_ref, other_ref), extra_refs = refs[:3], refs[3 : 3 + len(extra)]
        refs = refs[3 + len(extra) + len(earlier) :]
        outs, refs = refs[: len(shapes)], refs[len(shapes) :]
        low_outs, refs = refs[: len(more)], refs[len(more) :]
        bufs, (act, turned, grad, act_sems, grad_sems, out_sems) = refs[:6], refs[6:]
        step = pl.program_id(0)

        def act_copy(part):
            place = choice_ref[0] if part == 0 else 1 - choice_ref[0]
            return pltpu.make_async_copy(
                act_ref.at[pl.ds(pl.multiple_of(place * half, half), half)],
                act.at[pl.ds(part * half, half)],
                act_sems.at[part],
            )

        def fill(buf, pair, numbers):
            if not extra:
                return
            buf[features:] = jnp.zeros((below, buf.shape[1]), jnp.bfloat16)
            first = features
            for ref in extra_refs:
                size = ref.shape[1]
                place = pl.ds(pl.multiple_of(first + choice_ref[1] * size, size), size)
                for number in numbers:
                    column = 0 if len(numbers) == 1 else number * cut
                    value = adapter_scale_factor * ref[choice_ref[2 + 2 * pair + number]]
                    buf[place, column : column + cut] = value.astype(jnp.bfloat16)
                first += CUSTOMER_COUNT * size

        def grad_copy(number, part):
            columns = pl.ds(pl.multiple_of(choice_ref[2 + number] * cut, cut), cut)
            return pltpu.make_async_copy(
                (own_ref, other_ref)[part].at[:, columns],
                grad.at[number // 2, pl.ds(part * half, half), pl.ds(number % 2 * cut, cut)],
                grad_sems.at[number, part],
            )

        def out_copy(index):
            return pltpu.make_async_copy(bufs[index], outs[index], out_sems.at[index])

        @pl.when(step == 0)
        def _():
            for part in range(2):
                act_copy(part).start()
            for number in range(8):
                for part in range(2):
                    grad_copy(number, part).start()
            for part in range(2):
                act_copy(part).wait()
            turned[...] = act[...].T

        for pair in range(4):

            @pl.when(step == pair)
            def _():
                for number in (2 * pair, 2 * pair + 1):
                    for part in range(2):
                        grad_copy(number, part).wait()
                part = jnp.dot(turned[...], grad[pair], preferred_element_type=jnp.float32)
                for low_out in low_outs:
                    for number in range(2):
                        low_out[choice_ref[2 + 2 * pair + number]] = part[
                            features : features + rank, number * cut : (number + 1) * cut
                        ]
                part = part[:features].astype(jnp.bfloat16)
                if pair < 2:
                    bufs[pair][:features] = part
                    fill(bufs[pair], pair, (0, 1))
                    out_copy(pair).start()
                else:
                    for number in range(2):
                        index = 2 * pair - 2 + number
                        bufs[index][:features] = part[:, number * cut : (number + 1) * cut]
                        fill(bufs[index], pair, (number,))
                        out_copy(index).start()

        @pl.when(step == 3)
        def _():
            for index in range(6):
                out_copy(index).wait()

    return pl.pallas_call(
        body,
        grid_spec=pltpu.PrefetchScalarGridSpec(
            num_scalar_prefetch=1,
            grid=(4,),
            in_specs=anywhere(3)
            + [pl.BlockSpec(blocks.shape, lambda step, choice_ref: (0, 0, 0)) for blocks in extra]
            + anywhere(len(earlier)),
            out_specs=anywhere(len(shapes))
            + [pl.BlockSpec(shape, lambda step, choice_ref: (0, 0, 0)) for shape in more],
            scratch_shapes=[pltpu.VMEM(shape, jnp.bfloat16) for shape in shapes]
            + [
                pltpu.VMEM((2 * half, total), jnp.bfloat16),
                pltpu.VMEM((total, 2 * half), jnp.bfloat16),
                pltpu.VMEM((4, 2 * half, block), jnp.bfloat16),
                pltpu.SemaphoreType.DMA((2,)),
                pltpu.SemaphoreType.DMA((8, 2)),
                pltpu.SemaphoreType.DMA((6,)),
            ],
        ),
        out_shape=[jax.ShapeDtypeStruct(shape, jnp.bfloat16) for shape in shapes]
        + [jax.ShapeDtypeStruct(shape, jnp.float32) for shape in more],
        compiler_params=pltpu.CompilerParams(vmem_limit_bytes=VMEM_LIMIT),
        cost_estimate=cost(
            4 * half * total * hidden, 2 * (2 * half * (total + hidden) + total * hidden)
        ),
        name="weight_chunk",
    )(choice.astype(jnp.int32), act, own, other, *extra, *earlier)


def sums(terms, width, joined, earlier):
    rows = terms[0][0][0].shape[0]
    tile = next(size for size in (256, 320, 352, 224, rows) if rows % size == 0)
    arrays = [array for term in terms for array, _ in term]
    firsts = [first for term in terms for _, first in term]

    def spec(first):
        return pl.BlockSpec((tile, width), lambda step: (step, first // width))

    def body(*refs):
        refs, outs = refs[: len(arrays)], refs[len(arrays) + len(earlier) :]
        at = 0
        for index, term in enumerate(terms):
            total = refs[at][...].astype(jnp.float32)
            for ref in refs[at + 1 : at + len(term)]:
                total = total + ref[...].astype(jnp.float32)
            total = total.astype(jnp.bfloat16)
            if joined:
                outs[0][:, index * width : (index + 1) * width] = total
            else:
                outs[index][...] = total
            at += len(term)

    if joined:
        out_specs = [pl.BlockSpec((tile, width * len(terms)), lambda step: (step, 0))]
        out_shape = [jax.ShapeDtypeStruct((rows, width * len(terms)), jnp.bfloat16)]
    else:
        out_specs = [spec(0)] * len(terms)
        out_shape = [jax.ShapeDtypeStruct((rows, width), jnp.bfloat16)] * len(terms)
    return pl.pallas_call(
        body,
        grid=(rows // tile,),
        in_specs=[spec(first) for first in firsts] + anywhere(len(earlier)),
        out_specs=out_specs,
        out_shape=out_shape,
        compiler_params=pltpu.CompilerParams(vmem_limit_bytes=VMEM_LIMIT),
        cost_estimate=cost(0, 2 * rows * width * (len(arrays) + len(terms))),
        name="sums",
    )(*arrays, *earlier)


def assemble(whole, shape, span, pieces, group, earlier):
    start, stop = span
    width = pieces[0].shape[1]
    cut = width // 2
    tile = 256

    def body(group_ref, own_ref, near_ref, far_ref, low_ref, high_ref, *refs):
        out = refs[-1]
        for device in range(4):

            @pl.when(group_ref[0] == device)
            def _():
                for ref, other in ((own_ref, 0), (near_ref, 1), (far_ref, 2)):
                    begin = (device ^ other) * width
                    out[:, begin : begin + width] = ref[...]
                begin = (device ^ 3) * width
                out[:, begin : begin + cut] = low_ref[...]
                out[:, begin + cut : begin + width] = high_ref[...]

    extra = ([] if whole is None else [whole]) + list(earlier)
    return pl.pallas_call(
        body,
        grid_spec=pltpu.PrefetchScalarGridSpec(
            num_scalar_prefetch=1,
            grid=((stop - start) // tile,),
            in_specs=[
                pl.BlockSpec((tile, piece.shape[1]), lambda step, group_ref: (step, 0))
                for piece in pieces
            ]
            + anywhere(len(extra)),
            out_specs=pl.BlockSpec(
                (tile, shape[1]), lambda step, group_ref: (start // tile + step, 0)
            ),
        ),
        out_shape=jax.ShapeDtypeStruct(shape, pieces[0].dtype),
        input_output_aliases={} if whole is None else {1 + len(pieces): 0},
        compiler_params=pltpu.CompilerParams(vmem_limit_bytes=VMEM_LIMIT),
        cost_estimate=cost(0, 16 * (stop - start) * width),
        name="assemble",
    )(jnp.reshape(group, (1,)).astype(jnp.int32), *pieces, *extra)


def adapter_totals(pieces, first, size, group, earlier):
    width = pieces[0].shape[1]
    cut = width // 2

    def body(group_ref, own_ref, near_ref, far_ref, low_ref, high_ref, *refs):
        outs = refs[len(earlier) :]
        for device in range(4):

            @pl.when(group_ref[0] == device)
            def _():
                opposite = (device ^ 3) * width
                for ref, begin in (
                    (own_ref, device * width), (near_ref, (device ^ 1) * width),
                    (far_ref, (device ^ 2) * width), (low_ref, opposite),
                    (high_ref, opposite + cut),
                ):
                    for index, out in enumerate(outs):
                        at = first + index * size
                        value = ref[at : at + size].astype(jnp.float32)
                        out[:, begin : begin + ref.shape[1]] = value

    return pl.pallas_call(
        body,
        grid_spec=pltpu.PrefetchScalarGridSpec(
            num_scalar_prefetch=1,
            grid=(1,),
            in_specs=[
                pl.BlockSpec(piece.shape, lambda step, group_ref: (0, 0)) for piece in pieces
            ]
            + anywhere(len(earlier)),
            out_specs=[pl.BlockSpec((size, 4 * width), lambda step, group_ref: (0, 0))] * 2,
        ),
        out_shape=[jax.ShapeDtypeStruct((size, 4 * width), jnp.float32)] * 2,
        compiler_params=pltpu.CompilerParams(vmem_limit_bytes=VMEM_LIMIT),
        cost_estimate=cost(0, 48 * size * width),
        name="adapter_totals",
    )(jnp.reshape(group, (1,)).astype(jnp.int32), *pieces, *earlier)


def input_part(slots, rows, own, other, weight, down, up, given, begin, end, earlier):
    half, hidden = own.shape
    features = weight.shape[0]
    rank = up.shape[0]
    tile = 512
    first = begin // tile
    low_shapes = [] if given else [(2 * half, 3 * rank)] + [(rows, rank)] * 4

    def body(slots_ref, own_ref, other_ref, weight_ref, down_ref, up_ref, *refs):
        low, refs = refs[0], refs[len(given) + len(earlier) :]
        out, refs, (grad, rounded, sems) = refs[0], refs[1:-3], refs[-3:]
        if not given:
            low, low_outs = refs[0], refs[1:]

        @pl.when(pl.program_id(0) == 0)
        def _():
            copies = [
                pltpu.make_async_copy(
                    ref, grad.at[pl.ds(index * half, half)], sems.at[index]
                )
                for index, ref in enumerate((own_ref, other_ref))
            ]
            for copy in copies:
                copy.start()
            for copy in copies:
                copy.wait()
            if given:
                return
            part = lax.dot_general(
                grad[...], up_ref[...], (((1,), (1,)), ((), ())),
                preferred_element_type=jnp.float32,
            )
            rounded[...] = part.astype(jnp.bfloat16)
            for index, low_out in enumerate(low_outs):
                start = pl.multiple_of(slots_ref[1 + index] * rows, rows)
                low_out[...] = rounded[pl.ds(start, rows), :]
            part = adapter_scale_factor * part
            high = part.astype(jnp.bfloat16)
            rest = part - high.astype(jnp.float32)
            middle = rest.astype(jnp.bfloat16)
            rest = rest - middle.astype(jnp.float32)
            low[:, :rank] = high
            low[:, rank : 2 * rank] = middle
            low[:, 2 * rank :] = rest.astype(jnp.bfloat16)

        total = lax.dot_general(
            grad[...], weight_ref[...], (((1,), (1,)), ((), ())),
            preferred_element_type=jnp.float32,
        )
        downs = jnp.concatenate([down_ref[...]] * 3, axis=0)
        total = total + jnp.dot(low[...], downs, preferred_element_type=jnp.float32)
        total = total.astype(jnp.bfloat16)
        core = slots_ref[0]
        out[pl.ds(pl.multiple_of(core * half, half), half), :] = total[:half]
        out[pl.ds(pl.multiple_of((1 - core) * half, half), half), :] = total[half:]

    return pl.pallas_call(
        body,
        grid_spec=pltpu.PrefetchScalarGridSpec(
            num_scalar_prefetch=1,
            grid=((end - begin) // tile,),
            in_specs=anywhere(2)
            + [
                pl.BlockSpec((tile, hidden), lambda step, slots_ref: (first + step, 0)),
                pl.BlockSpec((rank, tile), lambda step, slots_ref: (0, first + step)),
                pl.BlockSpec((rank, hidden), lambda step, slots_ref: (0, 0)),
            ]
            + [pl.BlockSpec(value.shape, lambda step, slots_ref: (0, 0)) for value in given[:1]]
            + anywhere(len(given[1:]) + len(earlier)),
            out_specs=[pl.BlockSpec((2 * half, tile), lambda step, slots_ref: (0, first + step))]
            + [pl.BlockSpec(shape, lambda step, slots_ref: (0, 0)) for shape in low_shapes],
            scratch_shapes=[
                pltpu.VMEM((2 * half, hidden), jnp.bfloat16),
                pltpu.VMEM((2 * half, rank), jnp.bfloat16),
                pltpu.SemaphoreType.DMA((2,)),
            ],
        ),
        out_shape=[
            jax.ShapeDtypeStruct(shape, jnp.bfloat16)
            for shape in [(2 * half, features)] + low_shapes
        ],
        input_output_aliases={7: 0} if given else {},
        compiler_params=pltpu.CompilerParams(vmem_limit_bytes=VMEM_LIMIT),
        cost_estimate=cost(
            4 * half * (end - begin) * hidden,
            2 * ((end - begin) * hidden + 2 * half * (hidden + end - begin)),
        ),
        name="input_part",
    )(slots.astype(jnp.int32), own, other, weight, down, up, *given, *earlier)


def low_term(low, places, gathered, source, earlier):
    rows, rank = low.shape
    width = source.shape[1]
    last = gathered.shape[1] // 128 - 1

    def body(places_ref, low_ref, *refs):
        total = low_ref[...].astype(jnp.float32)
        for index in range(3):
            columns = slice((index + 1) * rank, (index + 2) * rank)
            total = total + refs[index][:, columns].astype(jnp.float32)
        total = lax.dot_general(
            total.astype(jnp.bfloat16), refs[3][...], (((0,), (0,)), ((), ())),
            preferred_element_type=jnp.float32,
        )
        refs[-1][...] = total.astype(jnp.bfloat16)

    def block(index):
        return pl.BlockSpec((rows, 128), lambda step, places_ref: (places_ref[index], last))

    return pl.pallas_call(
        body,
        grid_spec=pltpu.PrefetchScalarGridSpec(
            num_scalar_prefetch=1,
            grid=(1,),
            in_specs=[pl.BlockSpec(low.shape, lambda step, places_ref: (0, 0))]
            + [block(index) for index in range(3)]
            + [pl.BlockSpec(source.shape, lambda step, places_ref: (0, 0))]
            + anywhere(len(earlier)),
            out_specs=pl.BlockSpec((rank, width), lambda step, places_ref: (0, 0)),
        ),
        out_shape=jax.ShapeDtypeStruct((rank, width), jnp.bfloat16),
        compiler_params=pltpu.CompilerParams(vmem_limit_bytes=VMEM_LIMIT),
        cost_estimate=cost(2 * rank * source.size, 2 * source.size),
        name="low_term",
    )(places.astype(jnp.int32), low, gathered, gathered, gathered, source, *earlier)


def blocks_of(first, second, earlier):
    rank, width = first.shape
    cut = width // 8

    def body(first_ref, second_ref, *refs):
        for index in range(8):
            columns = slice(index * cut, (index + 1) * cut)
            refs[-1][index] = first_ref[:, columns].astype(jnp.float32) + second_ref[
                :, columns
            ].astype(jnp.float32)

    return pl.pallas_call(
        body,
        grid=(1,),
        in_specs=[pl.BlockSpec((rank, width), lambda step: (0, 0))] * 2 + anywhere(len(earlier)),
        out_specs=pl.BlockSpec((8, rank, cut), lambda step: (0, 0, 0)),
        out_shape=jax.ShapeDtypeStruct((8, rank, cut), jnp.float32),
        compiler_params=pltpu.CompilerParams(vmem_limit_bytes=VMEM_LIMIT),
        cost_estimate=cost(0, 8 * rank * width),
        name="blocks_of",
    )(first, second, *earlier)


def fast(
    activations, cotangent, preact, weight, adapter_input_weight, adapter_output_weight, owner
):
    group = lax.axis_index("dp")
    row = lax.axis_index("row")
    col = lax.axis_index("col")
    near, far = group % 2, group // 2
    client_index = owner[group]
    down = lax.dynamic_index_in_dim(adapter_input_weight, client_index, 0, keepdims=False)
    up = lax.dynamic_index_in_dim(adapter_output_weight, client_index, 0, keepdims=False)
    rows, features = activations.shape
    half, hidden = cotangent.shape
    rank = up.shape[0]
    wide = jnp.float32
    narrow = jnp.bfloat16

    def along(axis, pairs):
        return lambda value: lax.ppermute(value, axis, pairs)

    over_near = along("dp", [(i, i ^ 1) for i in range(4)])
    over_far = along("dp", [(i, i ^ 2) for i in range(4)])
    swap = along("col", [(0, 1), (1, 0)])

    bounds = [0]
    for part in CHUNKS:
        bounds.append(bounds[-1] + features * part // sum(CHUNKS))
    spans = list(zip(bounds[:-1], bounds[1:]))

    def at(shift):
        return (row + shift + 2 * col) % 4

    cuts, acts = {}, {}

    def cut_chunk(index, more, *earlier):
        begin, end = spans[index]
        cuts[index], one = cut_columns(activations, begin, end - begin, more, earlier)
        acts[index] = lax.all_gather(cuts[index], "row", axis=0, tiled=True)
        return one[0, 0]

    one = cut_chunk(0, [])
    cut_chunk(1, [], cuts[0])

    own = (cotangent.astype(wide) * gelu_slope(preact.astype(wide)) * one).astype(narrow)
    other = swap(own)

    over_last = (((1,), (1,)), ((), ()))
    low_act = lax.dot_general(activations, down, over_last, preferred_element_type=wide)
    low_act = low_act.astype(narrow)
    low_act = (low_act.astype(wide) + swap(low_act).astype(wide)).astype(narrow)

    cut = hidden // 8

    def first_kind(a, b):
        return 2 * (a + 2 * b)

    def second_kind(a, b):
        return 2 * (a + 2 * b) + 1

    blocks = jnp.stack([
        first_kind(1 - near, 1 - far), first_kind(1 - near, far),
        second_kind(1 - near, 1 - far), second_kind(near, 1 - far),
        first_kind(near, 1 - far), first_kind(near, far),
        second_kind(1 - near, far), second_kind(near, far),
    ])

    out_term = []
    first, got, kept, sent, more, done, spread, passed = {}, {}, {}, {}, {}, {}, {}, {}
    grad_weight = [None]

    choice = jnp.concatenate([jnp.stack([col, client_index]), blocks])

    def start(index, extra, *earlier):
        begin, end = spans[index]
        to_near, to_far, *kept[index] = weight_chunk(
            choice, acts[index], own, other, end - begin, rank if index == LOW_CHUNK else 0,
            extra, earlier,
        )
        if index == LOW_CHUNK:
            out_term.append(kept[index].pop())
        first[index] = [to_near, to_far]
        got[index] = [over_near(to_near), over_far(to_far)]

    def second(index, *earlier):
        (got_near, got_far), (send_near, _, send_far, _) = got[index], kept[index]
        sent[index] = sums(
            [[(send_near, 0), (got_near, 0)], [(send_far, 0), (got_far, 0)]], cut, False, earlier
        )
        more[index] = [over_far(sent[index][0]), over_near(sent[index][1])]

    def third(index, *earlier):
        (got_near, got_far), (_, keep_near, _, keep_far) = got[index], kept[index]
        done[index] = sums(
            [
                [(keep_near, 0), (got_near, cut), (more[index][0], 0)],
                [(keep_far, 0), (got_far, cut), (more[index][1], 0)],
            ],
            cut, True, earlier,
        )
        (piece,) = done[index]
        spread[index] = [piece, over_near(piece), over_far(piece)]

    def forward(index, *earlier):
        _, from_near, from_far = spread[index]
        passed[index] = sums([[(from_far, 0)], [(from_near, cut)]], cut, False, earlier)
        spread[index] += [over_near(passed[index][0]), over_far(passed[index][1])]

    def finish(index, *earlier):
        grad_weight[0] = assemble(
            grad_weight[0], (features, hidden), spans[index], spread[index], group, earlier
        )

    slots = jnp.stack([col, at(0), at(1), at(2), at(3)])
    middle = features // 3
    grads, lows, *low_rows = input_part(
        slots, rows, own, other, weight, down, up, [], 0, middle, [cuts[1]]
    )
    start(0, [], grads)
    cut_chunk(LOW_CHUNK, [jnp.concatenate([low_act, *low_rows[1:]], axis=1)], first[0][0])
    cut_chunk(3, [], cuts[2])
    cut_chunk(4, [], cuts[3])
    second(0, cuts[4])
    third(0, *sent[0])
    start(1, [], *done[0])
    (grads,) = input_part(
        slots, rows, own, other, weight, down, up, [lows, grads], middle, features, first[1]
    )
    grad_input = lax.psum_scatter(grads, "row", scatter_dimension=0, tiled=True)
    forward(0, grads)
    second(1, *passed[0])
    third(1, *sent[1], *spread[0][3:])
    start(2, [], *done[1])
    finish(0, first[2][0])
    in_term = low_term(
        low_rows[0], jnp.stack([(row - shift) % 4 for shift in (1, 2, 3)]), acts[LOW_CHUNK],
        activations, [grad_weight[0]],
    )
    received = along("row", [(i, i ^ 1) for i in range(4)])(in_term)
    forward(1, in_term)
    second(2, *passed[1])
    third(2, *sent[2], *spread[1][3:])
    start(3, [], *done[2])
    finish(1, first[3][0])
    (in_term,) = sums([[(in_term, 0), (received, 0)]], features, False, [grad_weight[0]])
    received = along("row", [(i, i ^ 2) for i in range(4)])(in_term)
    forward(2, in_term)
    second(3, *passed[2])
    in_term = blocks_of(in_term, received, sent[3])
    third(3, in_term, *spread[2][3:])
    start(4, [in_term, out_term[0]], *done[3])
    finish(2, first[4][0])
    forward(3, grad_weight[0])
    second(4, *passed[3])
    third(4, *sent[4], *spread[3][3:])
    finish(3, *done[4])
    forward(4, grad_weight[0])
    finish(4, *passed[4])
    size = CUSTOMER_COUNT * rank
    begin, end = spans[4]
    totals = adapter_totals(spread[4], end - begin, size, group, [grad_weight[0]])
    totals = [total.reshape(CUSTOMER_COUNT, rank, -1) for total in totals]
    return grad_input, grad_weight[0], totals[0], totals[1]


def plain(
    activations, cotangent, preact, weight, adapter_input_weight, adapter_output_weight, owner
):
    client_index = owner[lax.axis_index("dp")]
    down = lax.dynamic_index_in_dim(adapter_input_weight, client_index, 0, keepdims=False)
    up = lax.dynamic_index_in_dim(adapter_output_weight, client_index, 0, keepdims=False)
    owner_mask = (jnp.arange(CUSTOMER_COUNT) == client_index).astype(jnp.float32)
    grad_pre = (cotangent.astype(jnp.float32) * gelu_slope(preact.astype(jnp.float32))).astype(
        jnp.bfloat16
    )
    grad = lax.all_gather(grad_pre, "col", axis=0, tiled=True)
    act = lax.all_gather(activations, "row", axis=0, tiled=True)
    low_part = jnp.dot(grad, up.T, preferred_element_type=jnp.float32)
    low_act = lax.psum(
        jnp.dot(act, down.T, preferred_element_type=jnp.float32).astype(jnp.bfloat16), "col"
    )
    out_term = adapter_scale_factor * jnp.dot(
        low_act.T, grad, preferred_element_type=jnp.float32
    )
    input_part = jnp.dot(grad, weight.T, preferred_element_type=jnp.float32)
    input_part = input_part + adapter_scale_factor * jnp.dot(
        low_part, down.astype(jnp.float32), precision=lax.Precision.HIGHEST
    )
    grad_input = lax.psum_scatter(
        input_part.astype(jnp.bfloat16), "row", scatter_dimension=0, tiled=True
    )
    low_grad = lax.psum(low_part.astype(jnp.bfloat16), "row")
    in_term = adapter_scale_factor * jnp.dot(low_grad.T, act, preferred_element_type=jnp.float32)
    in_slots = owner_mask[:, None, None] * in_term[None]
    out_slots = owner_mask[:, None, None] * out_term[None]
    in_total = lax.psum(in_slots.astype(jnp.bfloat16), "dp").astype(jnp.float32)
    out_total = lax.psum(out_slots.astype(jnp.bfloat16), "dp").astype(jnp.float32)
    weight_term = lax.dot_general(
        act, grad, (((0,), (0,)), ((), ())), preferred_element_type=jnp.float32
    )
    grad_weight = lax.psum(weight_term.astype(jnp.bfloat16), "dp")
    return grad_input, grad_weight, in_total, out_total


def solution(mesh):
    sizes = (mesh.shape["dp"], mesh.shape["row"], mesh.shape["col"])
    placed = (
        P(("dp", "row"), "col"),
        P(("dp", "col"), "row"),
        P(("dp", "col"), "row"),
        P("col", "row"),
        P(None, None, "col"),
        P(None, None, "row"),
        P(),
    )
    return jax.shard_map(
        fast if sizes == (4, 4, 2) else plain,
        mesh=mesh,
        in_specs=placed,
        out_specs=(
            P(("dp", "row"), "col"),
            P("col", "row"),
            P(None, None, "col"),
            P(None, None, "row"),
        ),
        check_vma=False,
    )
```
